128 devices in a mesh: tm: 64 (over z, y, x), col: 2 (over core).
Axes of the slice: x: 4, y: 4, z: 4, core: 2. Of those that a mesh axis runs over, the one named last changes fastest.
Arguments:
- diagonal_blocks: float32 [128, 512, 512], P('tm', 'col'), as said below
- upper_blocks: float32 [128, 512, 512], P('tm', 'col')
- right_sides: float32 [128, 512, 512], P('tm', 'col'), may hold values from -6 to 6
Outputs:
- reduced_blocks: float32 [128, 512, 512], P('tm', 'col')
- reduced_uppers: float32 [128, 512, 512], P('tm', 'col')
- reduced_sources: float32 [128, 512, 512], P('tm', 'col')
The draws below stay inside these ranges and needn't reach their ends.
Inputs may be any that keep to these rules, and one draw needn't show every extreme that they name: `diagonal_blocks`: every block is symmetric, and the block-tridiagonal matrix built from these blocks and upper_blocks is positive definite.
All inputs are finite; a program needn't handle non-finite values.
Results may differ from the reference program's by a relative error of at most 0.0001.
Values sent between devices are 32-bit elements; how exact they have to be, the bound alone decides.
No kernel may reach another device: no remote copies, remote signals or barrier semaphores. Data moves between devices by JAX's collectives and lax.ppermute only.
A program may use at most 64 MiB of HBM per device.

```python
import jax
import jax.numpy as jnp
from jax import lax

MODES = 512
SOURCES = 512
LEVELS = 2
ROWS = 128


def coupling_factor(key):
    phi_key = jax.random.fold_in(key, 11)
    entries = jnp.clip(jax.random.normal(phi_key, (ROWS, MODES, MODES), jnp.float32), -6.0, 6.0)
    return entries * (2.0 / jnp.sqrt(1.0 * MODES))


def draw_diagonal_blocks(key, part):
    factor = coupling_factor(key)
    dense_key = jax.random.fold_in(key, 23)
    height_key = jax.random.fold_in(key, 37)
    dense = jnp.clip(jax.random.normal(dense_key, (ROWS, MODES, MODES), jnp.float32), -6.0, 6.0)
    dense = dense * (2.0 / jnp.sqrt(1.0 * MODES))
    total = jnp.einsum('nab,ncb->nac', factor, factor, precision=lax.Precision.HIGHEST) + jnp.einsum('nab,ncb->nac', dense, dense, precision=lax.Precision.HIGHEST)
    total = 0.5 * (total + jnp.swapaxes(total, 1, 2))
    heights = jnp.exp(jax.random.uniform(height_key, (ROWS, MODES), jnp.float32, jnp.log(3.0), jnp.log(9.0)))
    return total + heights[:, :, None] * jnp.eye(MODES, dtype=jnp.float32)


def draw_upper_blocks(key, part):
    return -jnp.swapaxes(coupling_factor(key), 1, 2)


def block_levels(own_key, shape, pieces, least, top_value):
    gain = 1.0
    for axis_at, parts in pieces:
        draws = jax.random.uniform(jax.random.fold_in(jax.random.fold_in(own_key, 6), axis_at), (parts,), jnp.float32, least / len(pieces), top_value / len(pieces))
        gain = gain * jnp.repeat(jnp.exp(draws), shape[axis_at] // parts).reshape((-1,) + (1,) * (len(shape) - 1 - axis_at))
    return gain


def noise(own_key, dims, width, most, pieces=(), kind=jnp.bfloat16):
    result = jax.random.normal(own_key, dims, jnp.float32) * width
    if len(pieces) > 0:
        result = block_levels(own_key, dims, pieces, -0.22, 0.18) * result
    return jnp.clip(result, min=-most, max=most).astype(kind)


def setup_inputs(seed: int = 0) -> dict:
    streams_of = jax.random.split(jax.random.key(seed), 4)
    diagonal_blocks = draw_diagonal_blocks(jax.random.fold_in(streams_of[3], 71), 0)
    upper_blocks = draw_upper_blocks(jax.random.fold_in(streams_of[3], 71), 0)
    right_sides = noise(streams_of[2], (ROWS, SOURCES, MODES), 1.0, 6.0, ((0, 64), (1, 2)), jnp.float32)
    return dict(diagonal_blocks=diagonal_blocks, upper_blocks=upper_blocks, right_sides=right_sides)


HIGHEST = lax.Precision.HIGHEST

def solve_right(factor, values, transposed):
    return lax.linalg.triangular_solve(factor, values, left_side=False, lower=True, transpose_a=transposed)

def apply_inverse(factor, values):
    return solve_right(factor, solve_right(factor, values, True), False)

def product(pattern, left_operand, right_operand):
    return jnp.einsum(pattern, left_operand, right_operand, precision=HIGHEST)

def eliminate(pivot, coupling, onward, sources):
    factor = lax.linalg.cholesky(pivot)
    scaled = apply_inverse(factor, coupling)
    solved = apply_inverse(factor, sources)
    turned = apply_inverse(factor, jnp.swapaxes(onward, 1, 2))
    left_block = -product('nab,ncb->nac', scaled, coupling)
    left_source = -product('nkb,ncb->nkc', solved, coupling)
    right_block = -product('nab,nbc->nac', turned, onward)
    right_upper = -product('nab,nbc->nac', scaled, onward)
    right_source = -product('nkb,nbc->nkc', solved, onward)
    return (left_block, left_source, right_block, right_upper, right_source)

def shifted(values):
    return jnp.concatenate([jnp.zeros_like(values[:1]), values[:-1]], axis=0)

def reference(diagonal_blocks, upper_blocks, right_sides):
    blocks = diagonal_blocks
    uppers = upper_blocks
    sources = right_sides
    for level_index in range(LEVELS):
        stride = 2 ** level_index
        active_block = blocks[::stride]
        active_upper = uppers[::stride]
        active_source = sources[::stride]
        onward = jnp.concatenate([active_upper[2::2], jnp.zeros_like(active_upper[:1])], axis=0)
        left_block, left_source, right_block, right_upper, right_source = eliminate(active_block[1::2], active_upper[1::2], onward, active_source[1::2])
        kept_block = active_block[0::2] + left_block + shifted(right_block)
        kept_upper = jnp.concatenate([active_upper[:1], right_upper[:-1]], axis=0)
        kept_source = active_source[0::2] + left_source + shifted(right_source)
        blocks = blocks.at[::2 * stride].set(kept_block)
        uppers = uppers.at[::2 * stride].set(kept_upper)
        sources = sources.at[::2 * stride].set(kept_source)
    return (blocks, uppers, sources)
```

```python
import jax
import jax.numpy as jnp
from jax import lax
from jax.experimental import pallas as pl
from jax.experimental.pallas import tpu as pltpu
from jax.sharding import PartitionSpec as P

F32 = jnp.float32
BF16 = jnp.bfloat16
N = 512
H = N // 2

NN = (((1,), (0,)), ((), ()))
NT = (((1,), (1,)), ((), ()))
TN = (((0,), (0,)), ((), ()))

VMEM = pl.BlockSpec(memory_space=pltpu.VMEM)
SMEM = pl.BlockSpec(memory_space=pltpu.SMEM)

SQUARINGS = 5
TARGET = 3e-3
USABLE = 0.6


def dot(a, b, dims=NN):
    return lax.dot_general(a, b, dims, preferred_element_type=F32)


def halves(x):
    high = x.astype(BF16)
    return high, (x - high.astype(F32)).astype(BF16)


def dot3(a, b, dims=NN):
    (ah, al), (bh, bl) = a, b
    return dot(ah, bh, dims) + (dot(ah, bl, dims) + dot(al, bh, dims))


def identity():
    rows = lax.broadcasted_iota(jnp.int32, (N, N), 0)
    lanes = lax.broadcasted_iota(jnp.int32, (N, N), 1)
    return jnp.where(rows == lanes, 1.0, 0.0).astype(F32)


def sweep_inverse(d_ref, x_ref):
    x_ref[...] = d_ref[...]

    def step(k, carry):
        rows = lax.broadcasted_iota(jnp.int32, (N, N), 0)
        lanes = lax.broadcasted_iota(jnp.int32, (N, N), 1)
        a = x_ref[...]
        row = x_ref[pl.ds(k, 1), :]
        col = jnp.sum(jnp.where(lanes == k, a, 0.0), axis=1, keepdims=True)
        lane = lax.broadcasted_iota(jnp.int32, (1, N), 1)
        inv = 1.0 / jnp.sum(jnp.where(lane == k, row, 0.0), axis=1, keepdims=True)
        row = row * inv
        new = a - col * row
        new = jnp.where(rows == k, jnp.broadcast_to(row, (N, N)), new)
        new = jnp.where(lanes == k, jnp.broadcast_to(col * inv, (N, N)), new)
        new = jnp.where(jnp.logical_and(rows == k, lanes == k), -inv, new)
        x_ref[...] = new
        return carry

    lax.fori_loop(0, N, step, 0)
    x_ref[...] = -x_ref[...]


def invert(d_ref, x_ref, res_ref):
    block = d_ref[...]
    top = jnp.max(jnp.sum(jnp.abs(block), axis=1, keepdims=True), axis=0, keepdims=True)
    alpha = 1.9 / top
    r = identity() - block * alpha
    y = identity() + r
    r = r.astype(BF16)
    r = dot(r, r).astype(BF16)
    for _ in range(SQUARINGS - 1):
        squared = dot(r, r)
        y = y + dot(y.astype(BF16), r)
        r = squared.astype(BF16)
    y = y + dot(y.astype(BF16), r)
    x_ref[...] = y * alpha

    def measure():
        residual = identity() - dot3(halves(d_ref[...]), halves(x_ref[...]))
        res_ref[...] = residual
        return jnp.sum(residual * residual)

    def improve():
        x = x_ref[...]
        x_ref[...] = x + dot(x.astype(BF16), res_ref[...].astype(BF16))

    def going(carry):
        size, count = carry
        return (size > TARGET * TARGET) & (size < USABLE * USABLE) & (count < 6)

    def refine(carry):
        improve()
        return measure(), carry[1] + 1

    size, _ = lax.while_loop(going, refine, (measure(), 0))
    converged = size <= TARGET * TARGET

    @pl.when(converged)
    def _():
        improve()

    @pl.when(jnp.logical_not(converged))
    def _():
        sweep_inverse(d_ref, x_ref)


def join(info_ref, own_ref, other_ref, full_ref):
    core = info_ref[0]
    full_ref[pl.ds(pl.multiple_of(core * H, H), H), :] = own_ref[...]
    full_ref[pl.ds(pl.multiple_of((1 - core) * H, H), H), :] = other_ref[...]


def own_rows(info_ref, full_ref):
    return full_ref[pl.ds(pl.multiple_of(info_ref[0] * H, H), H), :]


def own_columns(info_ref, full_ref):
    return full_ref[:, pl.ds(pl.multiple_of(info_ref[0] * H, H), H)]


def call(kernel, outs, operands, scratch, flops, limit=32):
    moved = sum(o.size * 4 for o in operands) + sum(4 * jnp.zeros(o, F32).size for o in outs)
    return pl.pallas_call(
        kernel,
        out_shape=[jax.ShapeDtypeStruct(o, F32) for o in outs],
        in_specs=[SMEM] + [VMEM] * (len(operands) - 1),
        out_specs=[VMEM] * len(outs),
        scratch_shapes=[pltpu.VMEM(s, F32) for s in scratch],
        compiler_params=pltpu.CompilerParams(vmem_limit_bytes=limit * 2**20),
        cost_estimate=pl.CostEstimate(flops=flops, bytes_accessed=moved, transcendentals=0),
    )(*operands)


CUBE = 2 * N * N * N
FULL = (N, N)
SLAB = (H, N)
PAIR = (2, H, N)


def first_inverse(info, own, other):
    def kernel(info_ref, own_ref, other_ref, z_ref, zc_ref, d_ref, res_ref):
        join(info_ref, own_ref, other_ref, d_ref)
        invert(d_ref, z_ref, res_ref)
        zc_ref[...] = own_rows(info_ref, z_ref)

    return call(kernel, [FULL, SLAB], [info, own, other], [FULL, FULL], 20 * CUBE)


def left_updates(info, z, uo, uo_other, de, de_other, fe, fo):
    def kernel(info_ref, z_ref, uo_ref, uox_ref, de_ref, dex_ref, fe_ref, fo_ref, a_ref, b_ref, u_ref):
        join(info_ref, uo_ref, uox_ref, u_ref)
        join(info_ref, de_ref, dex_ref, a_ref)
        z2 = halves(z_ref[...])
        u2 = halves(u_ref[...])
        v = dot3(u2, z2)
        a_ref[...] = a_ref[...] - dot3(halves(v), u2, NT)
        g = dot3(halves(fo_ref[...]), z2)
        b_ref[...] = fe_ref[...] - dot3(halves(g), u2, NT)

    return call(
        kernel, [FULL, SLAB], [info, z, uo, uo_other, de, de_other, fe, fo], [FULL], 9 * CUBE
    )


def coupled_upper(info, zq, zq_other, ue, ue_other, uq):
    def kernel(info_ref, zq_ref, zqx_ref, ue_ref, uex_ref, uq_ref, un_ref, z_ref, u_ref):
        join(info_ref, zq_ref, zqx_ref, z_ref)
        join(info_ref, ue_ref, uex_ref, u_ref)
        v = dot3(halves(uq_ref[...]), halves(z_ref[...]))
        fresh = -dot3(halves(v), halves(u_ref[...]))
        un_ref[...] = jnp.where(info_ref[1] > 0, fresh, ue_ref[...])

    return call(kernel, [SLAB, FULL, FULL], [info, zq, zq_other, ue, ue_other, uq], [], 3 * CUBE)


def second_inverse(info, a, zq, u):
    def kernel(info_ref, a_ref, zq_ref, u_ref, dc_ref, z_ref, zc_ref, d_ref, res_ref):
        u2 = halves(u_ref[...])
        w = dot3(u2, halves(zq_ref[...]), TN)
        d_ref[...] = a_ref[...] - dot3(halves(w), u2)
        dc_ref[...] = own_rows(info_ref, d_ref)

        @pl.when(info_ref[2] > 0)
        def _():
            invert(d_ref, z_ref, res_ref)
            zc_ref[...] = own_rows(info_ref, z_ref)

    return call(kernel, [SLAB, FULL, SLAB], [info, a, zq, u], [FULL, FULL], 26 * CUBE)


def level0_sources(info, b, fq, zq, u):
    def kernel(info_ref, b_ref, fq_ref, zq_ref, u_ref, f_ref):
        g = dot3(halves(fq_ref[...]), halves(zq_ref[...]))
        f_ref[...] = b_ref[...] - dot3(halves(g), halves(u_ref[...]))

    return call(kernel, [SLAB], [info, b, fq, zq, u], [], 3 * CUBE)[0]


def solved_sources(info, f, z):
    def kernel(info_ref, f_ref, z_ref, g_ref):
        @pl.when(info_ref[2] > 0)
        def _():
            g_ref[...] = dot3(halves(f_ref[...]), halves(z_ref[...]))

    return call(kernel, [SLAB], [info, f, z], [], CUBE)[0]


def level1_blocks(info, d, u_mid, u_mid_other, right, left, d_in, u_in):
    ur, urx, zr, zrx = right
    ul, zl, zlx = left

    def kernel(
        info_ref, d_ref, um_ref, umx_ref, ur_ref, urx_ref, zr_ref, zrx_ref, ul_ref, zl_ref, zlx_ref,
        din_ref, uin_ref, dout_ref, uout_ref, mid_ref, far_ref, zr_full, zl_full,
    ):
        dout_ref[1] = din_ref[1]
        uout_ref[1] = uin_ref[1]

        @pl.when(info_ref[2] > 0)
        def _():
            dout_ref[0] = d_ref[...]
            uout_ref[0] = um_ref[...]

        @pl.when(info_ref[2] == 0)
        def _():
            join(info_ref, um_ref, umx_ref, mid_ref)
            join(info_ref, ur_ref, urx_ref, far_ref)
            join(info_ref, zr_ref, zrx_ref, zr_full)
            join(info_ref, zl_ref, zlx_ref, zl_full)
            mid = halves(mid_ref[...])
            zl2 = halves(zl_full[...])
            v = dot3(halves(ur_ref[...]), halves(zr_full[...]))
            w = dot3(halves(own_columns(info_ref, mid_ref)), zl2, TN)
            dout_ref[0] = d_ref[...] - dot3(halves(v), halves(far_ref[...]), NT) - dot3(halves(w), mid)
            s = dot3(halves(ul_ref[...]), zl2)
            fresh = -dot3(halves(s), mid)
            uout_ref[0] = jnp.where(info_ref[1] > 0, fresh, um_ref[...])

    return call(
        kernel, [PAIR, PAIR],
        [info, d, u_mid, u_mid_other, ur, urx, zr, zrx, ul, zl, zlx, d_in, u_in],
        [FULL] * 4, 9 * CUBE,
    )


def level1_sources(info, f, gr, ur, urx, gl, u_mid, u_mid_other, f_in):
    def kernel(info_ref, f_ref, gr_ref, ur_ref, urx_ref, gl_ref, um_ref, umx_ref, fin_ref, out_ref, mid_ref, far_ref):
        out_ref[1] = fin_ref[1]

        @pl.when(info_ref[2] > 0)
        def _():
            out_ref[0] = f_ref[...]

        @pl.when(info_ref[2] == 0)
        def _():
            join(info_ref, um_ref, umx_ref, mid_ref)
            join(info_ref, ur_ref, urx_ref, far_ref)
            out_ref[0] = (
                f_ref[...]
                - dot3(halves(gr_ref[...]), halves(far_ref[...]), NT)
                - dot3(halves(gl_ref[...]), halves(mid_ref[...]))
            )

    return call(
        kernel, [PAIR], [info, f, gr, ur, urx, gl, u_mid, u_mid_other, f_in], [FULL, FULL], 3 * CUBE
    )[0]


def body(diagonal_blocks, upper_blocks, right_sides):
    chips = lax.axis_size("tm")
    position = lax.axis_index("tm")
    info = jnp.stack([lax.axis_index("col"), (position > 0).astype(jnp.int32), position % 2]).astype(jnp.int32)

    def swap(a):
        return lax.ppermute(a, "col", [(0, 1), (1, 0)])

    def onward(a):
        return lax.ppermute(a, "tm", [(i, i + 1) for i in range(chips - 1)])

    def odd_left(a):
        return lax.ppermute(a, "tm", [(i, i - 1) for i in range(1, chips, 2)])

    def odd_right(a):
        return lax.ppermute(a, "tm", [(i, i + 1) for i in range(1, chips - 1, 2)])

    de, do = diagonal_blocks[0], diagonal_blocks[1]
    ue, uo = upper_blocks[0], upper_blocks[1]
    fe, fo = right_sides[0], right_sides[1]

    uq = onward(uo)
    zo, zo_own = first_inverse(info, do, swap(do))
    zq = onward(zo_own)
    fq = onward(fo)
    a, b = left_updates(info, zo, uo, swap(uo), de, swap(de), fe, fo)
    u_mid, zq_full, ue_full = coupled_upper(info, zq, swap(zq), ue, swap(ue), uq)
    ur = odd_left(u_mid)
    ul = odd_right(u_mid)
    u_mid_other = swap(u_mid)
    d_mid, z1, z1_own = second_inverse(info, a, zq_full, ue_full)
    zr = odd_left(z1_own)
    zl = odd_right(z1_own)
    f_mid = level0_sources(info, b, fq, zq_full, ue_full)
    g1 = solved_sources(info, f_mid, z1)
    gr = odd_left(g1)
    gl = odd_right(g1)
    urx = swap(ur)
    d_out, u_out = level1_blocks(
        info, d_mid, u_mid, u_mid_other, (ur, urx, zr, swap(zr)), (ul, zl, swap(zl)),
        diagonal_blocks, upper_blocks,
    )
    f_out = level1_sources(info, f_mid, gr, ur, urx, gl, u_mid, u_mid_other, right_sides)
    return d_out, u_out, f_out


def solution(mesh):
    placed = (P("tm", "col", None),) * 3
    return jax.shard_map(body, mesh=mesh, in_specs=placed, out_specs=placed, check_vma=False)
```

```python
import jax
import jax.numpy as jnp
from jax import lax
from jax.experimental import pallas as pl
from jax.experimental.pallas import tpu as pltpu
from jax.sharding import PartitionSpec as P

F32 = jnp.float32
BF16 = jnp.bfloat16
N = 512
H = N // 2

NN = (((1,), (0,)), ((), ()))
NT = (((1,), (1,)), ((), ()))
TN = (((0,), (0,)), ((), ()))

VMEM = pl.BlockSpec(memory_space=pltpu.VMEM)
SMEM = pl.BlockSpec(memory_space=pltpu.SMEM)

SQUARINGS = 5
TARGET = 3e-3
USABLE = 0.6


def dot(a, b, dims=NN):
    return lax.dot_general(a, b, dims, preferred_element_type=F32)


def halves(x):
    high = x.astype(BF16)
    return high, (x - high.astype(F32)).astype(BF16)


def dot3(a, b, dims=NN):
    (ah, al), (bh, bl) = a, b
    return dot(ah, bh, dims) + (dot(ah, bl, dims) + dot(al, bh, dims))


def identity():
    rows = lax.broadcasted_iota(jnp.int32, (N, N), 0)
    lanes = lax.broadcasted_iota(jnp.int32, (N, N), 1)
    return jnp.where(rows == lanes, 1.0, 0.0).astype(F32)


def sweep_inverse(d_ref, x_ref):
    x_ref[...] = d_ref[...]

    def step(k, carry):
        rows = lax.broadcasted_iota(jnp.int32, (N, N), 0)
        lanes = lax.broadcasted_iota(jnp.int32, (N, N), 1)
        a = x_ref[...]
        row = x_ref[pl.ds(k, 1), :]
        col = jnp.sum(jnp.where(lanes == k, a, 0.0), axis=1, keepdims=True)
        lane = lax.broadcasted_iota(jnp.int32, (1, N), 1)
        inv = 1.0 / jnp.sum(jnp.where(lane == k, row, 0.0), axis=1, keepdims=True)
        row = row * inv
        new = a - col * row
        new = jnp.where(rows == k, jnp.broadcast_to(row, (N, N)), new)
        new = jnp.where(lanes == k, jnp.broadcast_to(col * inv, (N, N)), new)
        new = jnp.where(jnp.logical_and(rows == k, lanes == k), -inv, new)
        x_ref[...] = new
        return carry

    lax.fori_loop(0, N, step, 0)
    x_ref[...] = -x_ref[...]


def invert(d_ref, x_ref, res_ref):
    block = d_ref[...]
    top = jnp.max(jnp.sum(jnp.abs(block), axis=1, keepdims=True), axis=0, keepdims=True)
    alpha = 1.9 / top
    r = identity() - block * alpha
    y = identity() + r
    r = r.astype(BF16)
    r = dot(r, r).astype(BF16)
    for _ in range(SQUARINGS - 1):
        squared = dot(r, r)
        y = y + dot(y.astype(BF16), r)
        r = squared.astype(BF16)
    y = y + dot(y.astype(BF16), r)
    x_ref[...] = y * alpha

    def measure():
        residual = identity() - dot3(halves(d_ref[...]), halves(x_ref[...]))
        res_ref[...] = residual
        return jnp.sum(residual * residual)

    def improve():
        x = x_ref[...]
        x_ref[...] = x + dot(x.astype(BF16), res_ref[...].astype(BF16))

    def going(carry):
        size, count = carry
        return (size > TARGET * TARGET) & (size < USABLE * USABLE) & (count < 6)

    def refine(carry):
        improve()
        return measure(), carry[1] + 1

    size, _ = lax.while_loop(going, refine, (measure(), 0))
    converged = size <= TARGET * TARGET

    @pl.when(converged)
    def _():
        improve()

    @pl.when(jnp.logical_not(converged))
    def _():
        sweep_inverse(d_ref, x_ref)


def join(info_ref, own_ref, other_ref, full_ref):
    core = info_ref[0]
    full_ref[pl.ds(pl.multiple_of(core * H, H), H), :] = own_ref[...]
    full_ref[pl.ds(pl.multiple_of((1 - core) * H, H), H), :] = other_ref[...]


def own_rows(info_ref, full_ref):
    return full_ref[pl.ds(pl.multiple_of(info_ref[0] * H, H), H), :]


def own_columns(info_ref, full_ref):
    return full_ref[:, pl.ds(pl.multiple_of(info_ref[0] * H, H), H)]


B = 128
PACK = ((0, 0), (1, 0), (1, 1), (2, 0), (2, 1)), ((2, 2), (3, 0), (3, 1), (3, 2), (3, 3))
PACKED = (5 * B, B)


def pack(info_ref, full_ref, out_ref):
    for core in range(2):

        @pl.when(info_ref[0] == core)
        def _():
            for at, (i, j) in enumerate(PACK[core]):
                out_ref[at * B : (at + 1) * B, :] = full_ref[i * B : (i + 1) * B, j * B : (j + 1) * B]


def unpack(info_ref, own_ref, other_ref, full_ref):
    for core in range(2):

        @pl.when(info_ref[0] == core)
        def _():
            for half, ref in ((core, own_ref), (1 - core, other_ref)):
                for at, (i, j) in enumerate(PACK[half]):
                    block = ref[at * B : (at + 1) * B, :]
                    full_ref[i * B : (i + 1) * B, j * B : (j + 1) * B] = block
                    if i != j:
                        full_ref[j * B : (j + 1) * B, i * B : (i + 1) * B] = block.T


CUBE = 2 * N * N * N
FULL = (N, N)
SLAB = (H, N)
PAIR = (2, H, N)


def call(kernel, outs, operands, scratch, cubes, after=(), limit=32):
    count = len(operands)

    def entry(*refs):
        kernel(*refs[:count], *refs[count + len(after) :])

    return pl.pallas_call(
        entry,
        out_shape=[jax.ShapeDtypeStruct(o, F32) for o in outs],
        in_specs=[SMEM] + [VMEM] * (count - 1) + [pl.BlockSpec(memory_space=pl.ANY)] * len(after),
        out_specs=[VMEM] * len(outs),
        scratch_shapes=[pltpu.VMEM(s, F32) for s in scratch],
        compiler_params=pltpu.CompilerParams(vmem_limit_bytes=limit * 2**20),
        cost_estimate=pl.CostEstimate(
            flops=cubes * CUBE, bytes_accessed=(count + len(outs)) * 4 * H * N, transcendentals=0
        ),
    )(*operands, *after)


def first_inverse(info, own, other):
    def kernel(info_ref, own_ref, other_ref, z_ref, d_ref, res_ref):
        join(info_ref, own_ref, other_ref, d_ref)
        invert(d_ref, z_ref, res_ref)

    return call(kernel, [FULL], [info, own, other], [FULL, FULL], 20)[0]


def left_updates(info, z, uo, uo_other, de, de_other, fe, fo, after):
    def kernel(
        info_ref, z_ref, uo_ref, uox_ref, de_ref, dex_ref, fe_ref, fo_ref,
        a_ref, b_ref, v_ref, g_ref, zp_ref, u_ref,
    ):
        pack(info_ref, z_ref, zp_ref)
        join(info_ref, uo_ref, uox_ref, u_ref)
        join(info_ref, de_ref, dex_ref, a_ref)
        z2 = halves(z_ref[...])
        u2 = halves(u_ref[...])
        v = dot3(u2, z2)
        v_ref[...] = v
        a_ref[...] = a_ref[...] - dot3(halves(v), u2, NT)
        g = dot3(halves(fo_ref[...]), z2)
        g_ref[...] = g
        b_ref[...] = fe_ref[...] - dot3(halves(g), u2, NT)

    return call(
        kernel, [FULL, SLAB, FULL, SLAB, PACKED], [info, z, uo, uo_other, de, de_other, fe, fo],
        [FULL], 9, after,
    )


def coupled_upper(info, zq, zq_other, ue, ue_other, uq):
    def kernel(info_ref, zq_ref, zqx_ref, ue_ref, uex_ref, uq_ref, un_ref, z_ref, u_ref):
        unpack(info_ref, zq_ref, zqx_ref, z_ref)
        join(info_ref, ue_ref, uex_ref, u_ref)
        v = dot3(halves(uq_ref[...]), halves(z_ref[...]))
        fresh = -dot3(halves(v), halves(u_ref[...]))
        un_ref[...] = jnp.where(info_ref[1] > 0, fresh, ue_ref[...])

    return call(kernel, [SLAB, FULL, FULL], [info, zq, zq_other, ue, ue_other, uq], [], 3)


def second_inverse(info, a, zq, u):
    def kernel(info_ref, a_ref, zq_ref, u_ref, dc_ref, z_ref, zp_ref, d_ref, res_ref):
        u2 = halves(u_ref[...])
        w = dot3(u2, halves(zq_ref[...]), TN)
        d_ref[...] = a_ref[...] - dot3(halves(w), u2)
        dc_ref[...] = own_rows(info_ref, d_ref)

        @pl.when(info_ref[2] > 0)
        def _():
            invert(d_ref, z_ref, res_ref)
            pack(info_ref, z_ref, zp_ref)

    return call(kernel, [SLAB, FULL, PACKED], [info, a, zq, u], [FULL, FULL], 26)


def odd_sources(info, b, fq, zq, u, z, go, v, after):
    def kernel(
        info_ref, b_ref, fq_ref, zq_ref, u_ref, z_ref, go_ref, v_ref, f_ref, g_ref, gt_ref,
    ):
        @pl.when(info_ref[2] > 0)
        def _():
            gq = dot3(halves(fq_ref[...]), halves(zq_ref[...]))
            f = b_ref[...] - dot3(halves(gq), halves(u_ref[...]))
            f_ref[...] = f
            g = dot3(halves(f), halves(z_ref[...]))
            g_ref[...] = g
            gt_ref[...] = go_ref[...] - dot3(halves(g), halves(v_ref[...]))

        @pl.when(info_ref[2] == 0)
        def _():
            f_ref[...] = b_ref[...]

    return call(kernel, [SLAB, SLAB, SLAB], [info, b, fq, zq, u, z, go, v], [], 6, after)


def level1_blocks(info, d, u_mid, u_mid_other, right, left, d_in, u_in):
    ur, urx, zr, zrx = right
    ul, zl, zlx = left

    def kernel(
        info_ref, d_ref, um_ref, umx_ref, ur_ref, urx_ref, zr_ref, zrx_ref, ul_ref, zl_ref, zlx_ref,
        din_ref, uin_ref, dout_ref, uout_ref, mid_ref, far_ref, zr_full, zl_full,
    ):
        dout_ref[1] = din_ref[1]
        uout_ref[1] = uin_ref[1]

        @pl.when(info_ref[2] > 0)
        def _():
            dout_ref[0] = d_ref[...]
            uout_ref[0] = um_ref[...]

        @pl.when(info_ref[2] == 0)
        def _():
            join(info_ref, um_ref, umx_ref, mid_ref)
            join(info_ref, ur_ref, urx_ref, far_ref)
            unpack(info_ref, zr_ref, zrx_ref, zr_full)
            unpack(info_ref, zl_ref, zlx_ref, zl_full)
            mid = halves(mid_ref[...])
            zl2 = halves(zl_full[...])
            v = dot3(halves(ur_ref[...]), halves(zr_full[...]))
            w = dot3(halves(own_columns(info_ref, mid_ref)), zl2, TN)
            dout_ref[0] = d_ref[...] - dot3(halves(v), halves(far_ref[...]), NT) - dot3(halves(w), mid)
            s = dot3(halves(ul_ref[...]), zl2)
            fresh = -dot3(halves(s), mid)
            uout_ref[0] = jnp.where(info_ref[1] > 0, fresh, um_ref[...])

    return call(
        kernel, [PAIR, PAIR],
        [info, d, u_mid, u_mid_other, ur, urx, zr, zrx, ul, zl, zlx, d_in, u_in],
        [FULL] * 4, 9,
    )


def level1_sources(info, f, gr, ur, urx, gl, ue_full, f_in, after):
    def kernel(info_ref, f_ref, gr_ref, ur_ref, urx_ref, gl_ref, ue_ref, fin_ref, out_ref, far_ref):
        out_ref[1] = fin_ref[1]

        @pl.when(info_ref[2] > 0)
        def _():
            out_ref[0] = f_ref[...]

        @pl.when(info_ref[2] == 0)
        def _():
            join(info_ref, ur_ref, urx_ref, far_ref)
            out_ref[0] = (
                f_ref[...]
                - dot3(halves(gr_ref[...]), halves(far_ref[...]), NT)
                - dot3(halves(gl_ref[...]), halves(ue_ref[...]))
            )

    return call(kernel, [PAIR], [info, f, gr, ur, urx, gl, ue_full, f_in], [FULL], 3, after)[0]


def body(diagonal_blocks, upper_blocks, right_sides):
    chips = lax.axis_size("tm")
    position = lax.axis_index("tm")
    info = jnp.stack([lax.axis_index("col"), (position > 0).astype(jnp.int32), position % 2]).astype(jnp.int32)

    def swap(a):
        return lax.ppermute(a, "col", [(0, 1), (1, 0)])

    def onward(a, first=0, step=1):
        return lax.ppermute(a, "tm", [(i, i + 1) for i in range(first, chips - 1, step)])

    def odd_left(a):
        return lax.ppermute(a, "tm", [(i, i - 1) for i in range(1, chips, 2)])

    def odd_right(a):
        return onward(a, 1, 2)

    de, do = diagonal_blocks[0], diagonal_blocks[1]
    ue, uo = upper_blocks[0], upper_blocks[1]
    fe, fo = right_sides[0], right_sides[1]

    uq = onward(uo)
    zo = first_inverse(info, do, swap(do))
    a, b, vo, go, zo_packed = left_updates(info, zo, uo, swap(uo), de, swap(de), fe, fo, (uq,))
    zq = onward(zo_packed)
    fq = onward(fo, 0, 2)
    u_mid, zq_full, ue_full = coupled_upper(info, zq, swap(zq), ue, swap(ue), uq)
    ur = odd_left(u_mid)
    ul = odd_right(u_mid)
    u_mid_other = swap(u_mid)
    d_mid, z1, z1_packed = second_inverse(info, a, zq_full, ue_full)
    zr = odd_left(z1_packed)
    zl = odd_right(z1_packed)
    f_mid, g1, gt = odd_sources(info, b, fq, zq_full, ue_full, z1, go, vo, (ur, ul, u_mid_other))
    gr = odd_left(g1)
    gl = odd_right(gt)
    urx = swap(ur)
    d_out, u_out = level1_blocks(
        info, d_mid, u_mid, u_mid_other, (ur, urx, zr, swap(zr)), (ul, zl, swap(zl)),
        diagonal_blocks, upper_blocks,
    )
    f_out = level1_sources(info, f_mid, gr, ur, urx, gl, ue_full, right_sides, (d_out,))
    return d_out, u_out, f_out


def solution(mesh):
    placed = (P("tm", "col", None),) * 3
    return jax.shard_map(body, mesh=mesh, in_specs=placed, out_specs=placed, check_vma=False)
```

```python
import jax
import jax.numpy as jnp
from jax import lax
from jax.experimental import pallas as pl
from jax.experimental.pallas import tpu as pltpu
from jax.sharding import PartitionSpec as P

F32 = jnp.float32
BF16 = jnp.bfloat16
N = 512
H = N // 2

NN = (((1,), (0,)), ((), ()))
NT = (((1,), (1,)), ((), ()))
TN = (((0,), (0,)), ((), ()))

VMEM = pl.BlockSpec(memory_space=pltpu.VMEM)
SMEM = pl.BlockSpec(memory_space=pltpu.SMEM)

SQUARINGS = 5
TARGET = 3e-3
USABLE = 0.6


def dot(a, b, dims=NN):
    return lax.dot_general(a, b, dims, preferred_element_type=F32)


def halves(x):
    high = x.astype(BF16)
    return high, (x - high.astype(F32)).astype(BF16)


def dot3(a, b, dims=NN):
    (ah, al), (bh, bl) = a, b
    return dot(ah, bh, dims) + (dot(ah, bl, dims) + dot(al, bh, dims))


def identity():
    rows = lax.broadcasted_iota(jnp.int32, (N, N), 0)
    lanes = lax.broadcasted_iota(jnp.int32, (N, N), 1)
    return jnp.where(rows == lanes, 1.0, 0.0).astype(F32)


def sweep_inverse(d_ref, x_ref):
    x_ref[...] = d_ref[...]

    def step(k, carry):
        rows = lax.broadcasted_iota(jnp.int32, (N, N), 0)
        lanes = lax.broadcasted_iota(jnp.int32, (N, N), 1)
        a = x_ref[...]
        row = x_ref[pl.ds(k, 1), :]
        col = jnp.sum(jnp.where(lanes == k, a, 0.0), axis=1, keepdims=True)
        lane = lax.broadcasted_iota(jnp.int32, (1, N), 1)
        inv = 1.0 / jnp.sum(jnp.where(lane == k, row, 0.0), axis=1, keepdims=True)
        row = row * inv
        new = a - col * row
        new = jnp.where(rows == k, jnp.broadcast_to(row, (N, N)), new)
        new = jnp.where(lanes == k, jnp.broadcast_to(col * inv, (N, N)), new)
        new = jnp.where(jnp.logical_and(rows == k, lanes == k), -inv, new)
        x_ref[...] = new
        return carry

    lax.fori_loop(0, N, step, 0)
    x_ref[...] = -x_ref[...]


def invert(d_ref, x_ref, res_ref):
    block = d_ref[...]
    top = jnp.max(jnp.sum(jnp.abs(block), axis=1, keepdims=True), axis=0, keepdims=True)
    alpha = 1.9 / top
    r = identity() - block * alpha
    y = identity() + r
    r = r.astype(BF16)
    r = dot(r, r).astype(BF16)
    for _ in range(SQUARINGS - 1):
        squared = dot(r, r)
        y = y + dot(y.astype(BF16), r)
        r = squared.astype(BF16)
    y = y + dot(y.astype(BF16), r)
    x_ref[...] = y * alpha

    def measure():
        residual = identity() - dot3(halves(d_ref[...]), halves(x_ref[...]))
        res_ref[...] = residual
        return jnp.sum(residual * residual)

    def improve():
        x = x_ref[...]
        x_ref[...] = x + dot(x.astype(BF16), res_ref[...].astype(BF16))

    def going(carry):
        size, count = carry
        return (size > TARGET * TARGET) & (size < USABLE * USABLE) & (count < 6)

    def refine(carry):
        improve()
        return measure(), carry[1] + 1

    size, _ = lax.while_loop(going, refine, (measure(), 0))
    converged = size <= TARGET * TARGET

    @pl.when(converged)
    def _():
        improve()

    @pl.when(jnp.logical_not(converged))
    def _():
        sweep_inverse(d_ref, x_ref)


def join(info_ref, own_ref, other_ref, full_ref):
    core = info_ref[0]
    full_ref[pl.ds(pl.multiple_of(core * H, H), H), :] = own_ref[...]
    full_ref[pl.ds(pl.multiple_of((1 - core) * H, H), H), :] = other_ref[...]


def own_rows(info_ref, full_ref):
    return full_ref[pl.ds(pl.multiple_of(info_ref[0] * H, H), H), :]


def own_columns(info_ref, full_ref):
    return full_ref[:, pl.ds(pl.multiple_of(info_ref[0] * H, H), H)]


B = 128
PACK = ((0, 0), (1, 0), (1, 1), (2, 0), (2, 1)), ((2, 2), (3, 0), (3, 1), (3, 2), (3, 3))
PACKED = (5 * B, B)


def pack(info_ref, full_ref, out_ref):
    for core in range(2):

        @pl.when(info_ref[0] == core)
        def _():
            for at, (i, j) in enumerate(PACK[core]):
                out_ref[at * B : (at + 1) * B, :] = full_ref[i * B : (i + 1) * B, j * B : (j + 1) * B]


def unpack(info_ref, own_ref, other_ref, full_ref):
    for core in range(2):

        @pl.when(info_ref[0] == core)
        def _():
            for half, ref in ((core, own_ref), (1 - core, other_ref)):
                for at, (i, j) in enumerate(PACK[half]):
                    block = ref[at * B : (at + 1) * B, :]
                    full_ref[i * B : (i + 1) * B, j * B : (j + 1) * B] = block
                    if i != j:
                        full_ref[j * B : (j + 1) * B, i * B : (i + 1) * B] = block.T


CUBE = 2 * N * N * N
FULL = (N, N)
SLAB = (H, N)
PAIR = (2, H, N)


def call(kernel, outs, operands, scratch, cubes, after=(), rounded=(), limit=24):
    count = len(operands)
    outs = [(o, F32) for o in outs] + [(o, BF16) for o in rounded]

    def entry(*refs):
        kernel(*refs[:count], *refs[count + len(after) :])

    return pl.pallas_call(
        entry,
        out_shape=[jax.ShapeDtypeStruct(o, kind) for o, kind in outs],
        in_specs=[SMEM] + [VMEM] * (count - 1) + [pl.BlockSpec(memory_space=pl.ANY)] * len(after),
        out_specs=[VMEM] * len(outs),
        scratch_shapes=[pltpu.VMEM(s, F32) for s in scratch],
        compiler_params=pltpu.CompilerParams(vmem_limit_bytes=limit * 2**20),
        cost_estimate=pl.CostEstimate(
            flops=cubes * CUBE, bytes_accessed=(count + len(outs)) * 4 * H * N, transcendentals=0
        ),
    )(*operands, *after)


def first_inverse(info, d, d_other):
    def kernel(info_ref, own_ref, other_ref, z_ref, zp_ref, d_ref, res_ref):
        join(info_ref, own_ref.at[1], other_ref.at[1], d_ref)
        invert(d_ref, z_ref, res_ref)
        pack(info_ref, z_ref, zp_ref)

    return call(kernel, [FULL, PACKED], [info, d, d_other], [FULL, FULL], 20)


def left_updates(info, z, u, u_other, d, d_other, f, after):
    def kernel(info_ref, z_ref, u_ref, ux_ref, d_ref, dx_ref, f_ref, a_ref, b_ref, v_ref, g_ref, uo_ref):
        join(info_ref, u_ref.at[1], ux_ref.at[1], uo_ref)
        join(info_ref, d_ref.at[0], dx_ref.at[0], a_ref)
        z2 = halves(z_ref[...])
        u2 = halves(uo_ref[...])
        g = dot3(halves(f_ref[1]), z2)
        g_ref[...] = g
        b_ref[...] = f_ref[0] - dot3(halves(g), u2, NT)
        v = dot3(u2, z2)
        v_ref[...] = v
        a_ref[...] = a_ref[...] - dot3(halves(v), u2, NT)

    return call(
        kernel, [FULL, SLAB, FULL, SLAB], [info, z, u, u_other, d, d_other, f], [FULL], 9, after,
    )


def coupled_upper(info, zq, zq_other, u, u_other, uq):
    def kernel(info_ref, zq_ref, zqx_ref, ui_ref, uix_ref, uq_ref, un_ref, z_ref, u_ref):
        unpack(info_ref, zq_ref, zqx_ref, z_ref)
        join(info_ref, ui_ref.at[0], uix_ref.at[0], u_ref)
        v = dot3(halves(uq_ref[...]), halves(z_ref[...]))
        fresh = -dot3(halves(v), halves(u_ref[...]))
        un_ref[...] = jnp.where(info_ref[1] > 0, fresh, ui_ref[0])

    return call(kernel, [SLAB, FULL, FULL], [info, zq, zq_other, u, u_other, uq], [], 3)


def second_inverse(info, a, zq, u):
    def kernel(info_ref, a_ref, zq_ref, u_ref, dc_ref, z_ref, zp_ref, d_ref, res_ref):
        u2 = halves(u_ref[...])
        w = dot3(u2, halves(zq_ref[...]), TN)
        d_ref[...] = a_ref[...] - dot3(halves(w), u2)
        dc_ref[...] = own_rows(info_ref, d_ref)

        @pl.when(info_ref[2] > 0)
        def _():
            invert(d_ref, z_ref, res_ref)
            pack(info_ref, z_ref, zp_ref)

    return call(kernel, [SLAB, FULL, PACKED], [info, a, zq, u], [FULL, FULL], 26)


def odd_sources(info, b, gq, u, z, go, v, after):
    def kernel(info_ref, b_ref, gq_ref, u_ref, z_ref, go_ref, v_ref, f_ref, g_ref, gt_ref):
        @pl.when(info_ref[2] > 0)
        def _():
            f = b_ref[...] - dot3(halves(gq_ref[...]), halves(u_ref[...]))
            f_ref[...] = f
            g = dot3(halves(f), halves(z_ref[...]))
            g_ref[...] = g
            gt_ref[...] = go_ref[...] - dot3(halves(g), halves(v_ref[...]))

        @pl.when(info_ref[2] == 0)
        def _():
            f_ref[...] = b_ref[...]

    return call(kernel, [SLAB, SLAB, SLAB], [info, b, gq, u, z, go, v], [], 5, after)


def level1_blocks(info, d, u_mid, u_mid_other, right, left, ue, d_in, u_in):
    ur, urx, zr, zrx = right
    ul, zl, zlx = left

    def kernel(
        info_ref, d_ref, um_ref, umx_ref, ur_ref, urx_ref, zr_ref, zrx_ref, ul_ref, zl_ref, zlx_ref,
        ue_ref, din_ref, uin_ref, dout_ref, uout_ref, fh_ref, fl_ref, uh_ref, ul2_ref, mid_ref, far_ref, zr_full, zl_full,
    ):
        dout_ref[1] = din_ref[1]
        uout_ref[1] = uin_ref[1]

        @pl.when(info_ref[2] > 0)
        def _():
            dout_ref[0] = d_ref[...]
            uout_ref[0] = um_ref[...]

        @pl.when(info_ref[2] == 0)
        def _():
            join(info_ref, um_ref, umx_ref, mid_ref)
            join(info_ref, ur_ref, urx_ref, far_ref)
            unpack(info_ref, zr_ref, zrx_ref, zr_full)
            unpack(info_ref, zl_ref, zlx_ref, zl_full)
            far = halves(far_ref[...])
            fh_ref[...], fl_ref[...] = far
            uh_ref[...], ul2_ref[...] = halves(ue_ref[...])
            mid = halves(mid_ref[...])
            zl2 = halves(zl_full[...])
            v = dot3(halves(ur_ref[...]), halves(zr_full[...]))
            w = dot3(halves(own_columns(info_ref, mid_ref)), zl2, TN)
            dout_ref[0] = d_ref[...] - dot3(halves(v), far, NT) - dot3(halves(w), mid)
            s = dot3(halves(ul_ref[...]), zl2)
            fresh = -dot3(halves(s), mid)
            uout_ref[0] = jnp.where(info_ref[1] > 0, fresh, um_ref[...])

    return call(
        kernel, [PAIR, PAIR],
        [info, d, u_mid, u_mid_other, ur, urx, zr, zrx, ul, zl, zlx, ue, d_in, u_in],
        [FULL] * 4, 0, rounded=[FULL] * 4,
    )


def level1_sources(info, f, gr, gl, far, ue, f_in):
    def kernel(info_ref, f_ref, gr_ref, gl_ref, fh_ref, fl_ref, uh_ref, ul_ref, fin_ref, out_ref):
        out_ref[1] = fin_ref[1]

        @pl.when(info_ref[2] > 0)
        def _():
            out_ref[0] = f_ref[...]

        @pl.when(info_ref[2] == 0)
        def _():
            out_ref[0] = (
                f_ref[...]
                - dot3(halves(gr_ref[...]), (fh_ref[...], fl_ref[...]), NT)
                - dot3(halves(gl_ref[...]), (uh_ref[...], ul_ref[...]))
            )

    return call(kernel, [PAIR], [info, f, gr, gl, *far, *ue, f_in], [], 3)[0]


def body(diagonal_blocks, upper_blocks, right_sides):
    chips = lax.axis_size("tm")
    position = lax.axis_index("tm")
    info = jnp.stack([lax.axis_index("col"), (position > 0).astype(jnp.int32), position % 2]).astype(jnp.int32)

    def swap(a):
        return lax.ppermute(a, "col", [(0, 1), (1, 0)])

    def onward(a, first=0, step=1):
        return lax.ppermute(a, "tm", [(i, i + 1) for i in range(first, chips - 1, step)])

    def odd_left(a):
        return lax.ppermute(a, "tm", [(i, i - 1) for i in range(1, chips, 2)])

    def odd_right(a):
        return onward(a, 1, 2)

    d_other = swap(diagonal_blocks)
    uq = onward(upper_blocks[1])
    u_other = swap(upper_blocks)
    zo, zo_packed = first_inverse(info, diagonal_blocks, d_other)
    zq = onward(zo_packed)
    a, b, vo, go = left_updates(
        info, zo, upper_blocks, u_other, diagonal_blocks, d_other, right_sides, (uq,)
    )
    gq = onward(go, 0, 2)
    zq, a = lax.optimization_barrier((zq, a))
    u_mid, zq_full, ue_full = coupled_upper(info, zq, swap(zq), upper_blocks, u_other, uq)
    ur = odd_left(u_mid)
    ul = odd_right(u_mid)
    u_mid_other = swap(u_mid)
    d_mid, z1, z1_packed = second_inverse(info, a, zq_full, ue_full)
    zr = odd_left(z1_packed)
    zl = odd_right(z1_packed)
    f_mid, g1, gt = odd_sources(info, b, gq, ue_full, z1, go, vo, (ur, ul, u_mid_other))
    gr = odd_left(g1)
    gl = odd_right(gt)
    urx = swap(ur)
    d_out, u_out, fh, fl, uh, ul2 = level1_blocks(
        info, d_mid, u_mid, u_mid_other, (ur, urx, zr, swap(zr)), (ul, zl, swap(zl)), ue_full,
        diagonal_blocks, upper_blocks,
    )
    f_out = level1_sources(info, f_mid, gr, gl, (fh, fl), (uh, ul2), right_sides)
    return d_out, u_out, f_out


def solution(mesh):
    placed = (P("tm", "col", None),) * 3
    return jax.shard_map(body, mesh=mesh, in_specs=placed, out_specs=placed, check_vma=False)
```

```python
import jax
import jax.numpy as jnp
from jax import lax
from jax.experimental import pallas as pl
from jax.experimental.pallas import tpu as pltpu
from jax.sharding import PartitionSpec as P

F32 = jnp.float32
BF16 = jnp.bfloat16
N = 512
H = N // 2

NN = (((1,), (0,)), ((), ()))
NT = (((1,), (1,)), ((), ()))
TN = (((0,), (0,)), ((), ()))

VMEM = pl.BlockSpec(memory_space=pltpu.VMEM)
SMEM = pl.BlockSpec(memory_space=pltpu.SMEM)

SQUARINGS = 4
TARGET = 3e-3
USABLE = 0.6


def dot(a, b, dims=NN):
    return lax.dot_general(a, b, dims, preferred_element_type=F32)


def halves(x):
    high = x.astype(BF16)
    return high, (x - high.astype(F32)).astype(BF16)


def dot3(a, b, dims=NN):
    (ah, al), (bh, bl) = a, b
    return dot(ah, bh, dims) + (dot(ah, bl, dims) + dot(al, bh, dims))


def identity():
    rows = lax.broadcasted_iota(jnp.int32, (N, N), 0)
    lanes = lax.broadcasted_iota(jnp.int32, (N, N), 1)
    return jnp.where(rows == lanes, 1.0, 0.0).astype(F32)


def sweep_inverse(d_ref, x_ref):
    x_ref[...] = d_ref[...]

    def step(k, carry):
        rows = lax.broadcasted_iota(jnp.int32, (N, N), 0)
        lanes = lax.broadcasted_iota(jnp.int32, (N, N), 1)
        a = x_ref[...]
        row = x_ref[pl.ds(k, 1), :]
        col = jnp.sum(jnp.where(lanes == k, a, 0.0), axis=1, keepdims=True)
        lane = lax.broadcasted_iota(jnp.int32, (1, N), 1)
        inv = 1.0 / jnp.sum(jnp.where(lane == k, row, 0.0), axis=1, keepdims=True)
        row = row * inv
        new = a - col * row
        new = jnp.where(rows == k, jnp.broadcast_to(row, (N, N)), new)
        new = jnp.where(lanes == k, jnp.broadcast_to(col * inv, (N, N)), new)
        new = jnp.where(jnp.logical_and(rows == k, lanes == k), -inv, new)
        x_ref[...] = new
        return carry

    lax.fori_loop(0, N, step, 0)
    x_ref[...] = -x_ref[...]


def invert(d_ref, x_ref, res_ref):
    block = d_ref[...]
    low = block.astype(BF16)
    square = dot(low, low)
    top = jnp.max(jnp.sum(jnp.abs(square), axis=1, keepdims=True), axis=0, keepdims=True)
    alpha = 1.9 * lax.rsqrt(top)
    scaled = block * alpha
    y = 2.0 * identity() - scaled
    r = (y - scaled + square * (alpha * alpha) - identity()).astype(BF16)
    for _ in range(SQUARINGS - 1):
        squared = dot(r, r)
        y = y + dot(y.astype(BF16), r)
        r = squared.astype(BF16)
    y = y + dot(y.astype(BF16), r)
    start = (y * alpha).astype(BF16)
    high, rest = halves(d_ref[...])
    residual = identity() - (dot(high, start) + dot(rest, start))
    res_ref[...] = residual
    x_ref[...] = start.astype(F32)
    first = jnp.sum(residual * residual)

    def measure():
        residual = identity() - dot3(halves(d_ref[...]), halves(x_ref[...]))
        res_ref[...] = residual
        return jnp.sum(residual * residual)

    def improve():
        x = x_ref[...]
        x_ref[...] = x + dot(x.astype(BF16), res_ref[...].astype(BF16))

    def going(carry):
        size, count = carry
        return (size > TARGET * TARGET) & (size < USABLE * USABLE) & (count < 6)

    def refine(carry):
        improve()
        return measure(), carry[1] + 1

    size, _ = lax.while_loop(going, refine, (first, 0))
    converged = size <= TARGET * TARGET

    @pl.when(converged)
    def _():
        improve()

    @pl.when(jnp.logical_not(converged))
    def _():
        sweep_inverse(d_ref, x_ref)


def join(info_ref, own_ref, other_ref, full_ref):
    core = info_ref[0]
    full_ref[pl.ds(pl.multiple_of(core * H, H), H), :] = own_ref[...]
    full_ref[pl.ds(pl.multiple_of((1 - core) * H, H), H), :] = other_ref[...]


def own_rows(info_ref, full_ref):
    return full_ref[pl.ds(pl.multiple_of(info_ref[0] * H, H), H), :]


def own_columns(info_ref, full_ref):
    return full_ref[:, pl.ds(pl.multiple_of(info_ref[0] * H, H), H)]


B = 128
PACK = ((0, 0), (1, 0), (1, 1), (2, 0), (2, 1)), ((2, 2), (3, 0), (3, 1), (3, 2), (3, 3))
PACKED = (5 * B, B)


def pack(info_ref, full_ref, out_ref):
    for core in range(2):

        @pl.when(info_ref[0] == core)
        def _():
            for at, (i, j) in enumerate(PACK[core]):
                out_ref[at * B : (at + 1) * B, :] = full_ref[i * B : (i + 1) * B, j * B : (j + 1) * B]


def unpack(info_ref, own_ref, other_ref, full_ref):
    for core in range(2):

        @pl.when(info_ref[0] == core)
        def _():
            for half, ref in ((core, own_ref), (1 - core, other_ref)):
                for at, (i, j) in enumerate(PACK[half]):
                    block = ref[at * B : (at + 1) * B, :]
                    full_ref[i * B : (i + 1) * B, j * B : (j + 1) * B] = block
                    if i != j:
                        full_ref[j * B : (j + 1) * B, i * B : (i + 1) * B] = block.T


CUBE = 2 * N * N * N
FULL = (N, N)
SLAB = (H, N)
PAIR = (2, H, N)


def call(kernel, outs, operands, scratch, cubes, after=(), rounded=(), limit=24):
    count = len(operands)
    outs = [(o, F32) for o in outs] + [(o, BF16) for o in rounded]

    def entry(*refs):
        kernel(*refs[:count], *refs[count + len(after) :])

    return pl.pallas_call(
        entry,
        out_shape=[jax.ShapeDtypeStruct(o, kind) for o, kind in outs],
        in_specs=[SMEM] + [VMEM] * (count - 1) + [pl.BlockSpec(memory_space=pl.ANY)] * len(after),
        out_specs=[VMEM] * len(outs),
        scratch_shapes=[pltpu.VMEM(s, F32) for s in scratch],
        compiler_params=pltpu.CompilerParams(vmem_limit_bytes=limit * 2**20),
        cost_estimate=pl.CostEstimate(
            flops=cubes * CUBE, bytes_accessed=(count + len(outs)) * 4 * H * N, transcendentals=0
        ),
    )(*operands, *after)


def first_inverse(info, d, d_other):
    def kernel(info_ref, own_ref, other_ref, z_ref, zp_ref, d_ref, res_ref):
        join(info_ref, own_ref.at[1], other_ref.at[1], d_ref)
        invert(d_ref, z_ref, res_ref)
        pack(info_ref, z_ref, zp_ref)

    return call(kernel, [FULL, PACKED], [info, d, d_other], [FULL, FULL], 20)


def left_updates(info, z, u, u_other, d, d_other, f, after):
    def kernel(info_ref, z_ref, u_ref, ux_ref, d_ref, dx_ref, f_ref, a_ref, b_ref, v_ref, g_ref, uo_ref):
        join(info_ref, u_ref.at[1], ux_ref.at[1], uo_ref)
        join(info_ref, d_ref.at[0], dx_ref.at[0], a_ref)
        z2 = halves(z_ref[...])
        u2 = halves(uo_ref[...])
        g = dot3(halves(f_ref[1]), z2)
        g_ref[...] = g
        b_ref[...] = f_ref[0] - dot3(halves(g), u2, NT)
        v = dot3(u2, z2)
        v_ref[...] = v
        a_ref[...] = a_ref[...] - dot3(halves(v), u2, NT)

    return call(
        kernel, [FULL, SLAB, FULL, SLAB], [info, z, u, u_other, d, d_other, f], [FULL], 9, after,
    )


def coupled_upper(info, zq, zq_other, u, u_other, uq):
    def kernel(info_ref, zq_ref, zqx_ref, ui_ref, uix_ref, uq_ref, un_ref, t_ref, u_ref, z_ref):
        @pl.when(info_ref[2] > 0)
        def _():
            unpack(info_ref, zq_ref, zqx_ref, z_ref)
            join(info_ref, ui_ref.at[0], uix_ref.at[0], u_ref)
            t = dot3(halves(z_ref[...]), halves(u_ref[...]))
            t_ref[...] = t
            un_ref[...] = -dot3(halves(uq_ref[...]), halves(t))

    return call(kernel, [SLAB, FULL, FULL], [info, zq, zq_other, u, u_other, uq], [FULL], 3)


def second_inverse(info, a, t, u_full, zq, zq_other, u, u_other, uq, uq_other):
    def kernel(
        info_ref, a_ref, t_ref, u_ref, zq_ref, zqx_ref, ui_ref, uix_ref, uq_ref, uqx_ref,
        dc_ref, un_ref, z_ref, zp_ref, d_ref, res_ref,
    ):
        @pl.when(info_ref[2] > 0)
        def _():
            d_ref[...] = a_ref[...] - dot3(halves(u_ref[...]), halves(t_ref[...]), TN)
            dc_ref[...] = own_rows(info_ref, d_ref)
            invert(d_ref, z_ref, res_ref)
            pack(info_ref, z_ref, zp_ref)

        @pl.when(info_ref[2] == 0)
        def _():
            unpack(info_ref, zq_ref, zqx_ref, z_ref)
            join(info_ref, ui_ref.at[0], uix_ref.at[0], d_ref)
            t = halves(dot3(halves(z_ref[...]), halves(d_ref[...])))
            join(info_ref, uq_ref, uqx_ref, z_ref)
            un_ref[...] = jnp.where(info_ref[1] > 0, -dot3(halves(z_ref[...]), t), d_ref[...])
            dc_ref[...] = own_rows(info_ref, a_ref) - dot3(halves(own_columns(info_ref, d_ref)), t, TN)

    return call(
        kernel, [SLAB, FULL, FULL, PACKED], [info, a, t, u_full, zq, zq_other, u, u_other, uq, uq_other],
        [FULL, FULL], 24,
    )


def odd_sources(info, b, gq, u, z, go, v, after):
    def kernel(info_ref, b_ref, gq_ref, u_ref, z_ref, go_ref, v_ref, f_ref, g_ref, gt_ref):
        @pl.when(info_ref[2] > 0)
        def _():
            f = b_ref[...] - dot3(halves(gq_ref[...]), halves(u_ref[...]))
            f_ref[...] = f
            g = dot3(halves(f), halves(z_ref[...]))
            g_ref[...] = g
            gt_ref[...] = go_ref[...] - dot3(halves(g), halves(v_ref[...]))

        @pl.when(info_ref[2] == 0)
        def _():
            f_ref[...] = b_ref[...]

    return call(kernel, [SLAB, SLAB, SLAB], [info, b, gq, u, z, go, v], [], 5, after)


def level1_blocks(info, d, u_odd, mid, right, left, d_in, u_in, u_other):
    ur, urx, zr, zrx = right
    ul, zl, zlx = left

    def kernel(
        info_ref, d_ref, uo_ref, mid_ref, ur_ref, urx_ref, zr_ref, zrx_ref, ul_ref, zl_ref, zlx_ref,
        din_ref, uin_ref, uix_ref, dout_ref, uout_ref, fh_ref, fl_ref, uh_ref, uw_ref, far_ref, z_ref,
    ):
        dout_ref[1] = din_ref[1]
        uout_ref[1] = uin_ref[1]

        @pl.when(info_ref[2] > 0)
        def _():
            dout_ref[0] = d_ref[...]
            uout_ref[0] = uo_ref[...]

        @pl.when(info_ref[2] == 0)
        def _():
            join(info_ref, uin_ref.at[0], uix_ref.at[0], far_ref)
            uh_ref[...], uw_ref[...] = halves(far_ref[...])
            join(info_ref, ur_ref, urx_ref, far_ref)
            far = halves(far_ref[...])
            fh_ref[...], fl_ref[...] = far
            mid = halves(mid_ref[...])
            unpack(info_ref, zr_ref, zrx_ref, z_ref)
            v = dot3(halves(ur_ref[...]), halves(z_ref[...]))
            unpack(info_ref, zl_ref, zlx_ref, z_ref)
            z2 = halves(z_ref[...])
            w = dot3(halves(own_columns(info_ref, mid_ref)), z2, TN)
            dout_ref[0] = d_ref[...] - dot3(halves(v), far, NT) - dot3(halves(w), mid)
            s = dot3(halves(ul_ref[...]), z2)
            fresh = -dot3(halves(s), mid)
            uout_ref[0] = jnp.where(info_ref[1] > 0, fresh, own_rows(info_ref, mid_ref))

    return call(
        kernel, [PAIR, PAIR],
        [info, d, u_odd, mid, ur, urx, zr, zrx, ul, zl, zlx, d_in, u_in, u_other],
        [FULL] * 2, 0, rounded=[FULL] * 4,
    )


def level1_sources(info, f, gr, gl, far, ue, f_in):
    def kernel(info_ref, f_ref, gr_ref, gl_ref, fh_ref, fl_ref, uh_ref, ul_ref, fin_ref, out_ref):
        out_ref[1] = fin_ref[1]

        @pl.when(info_ref[2] > 0)
        def _():
            out_ref[0] = f_ref[...]

        @pl.when(info_ref[2] == 0)
        def _():
            out_ref[0] = (
                f_ref[...]
                - dot3(halves(gr_ref[...]), (fh_ref[...], fl_ref[...]), NT)
                - dot3(halves(gl_ref[...]), (uh_ref[...], ul_ref[...]))
            )

    return call(kernel, [PAIR], [info, f, gr, gl, *far, *ue, f_in], [], 3)[0]


def body(diagonal_blocks, upper_blocks, right_sides):
    chips = lax.axis_size("tm")
    position = lax.axis_index("tm")
    info = jnp.stack([lax.axis_index("col"), (position > 0).astype(jnp.int32), position % 2]).astype(jnp.int32)

    def swap(a):
        return lax.ppermute(a, "col", [(0, 1), (1, 0)])

    def onward(a, first=0, step=1):
        return lax.ppermute(a, "tm", [(i, i + 1) for i in range(first, chips - 1, step)])

    def odd_left(a):
        return lax.ppermute(a, "tm", [(i, i - 1) for i in range(1, chips, 2)])

    def odd_right(a):
        return onward(a, 1, 2)

    d_other = swap(diagonal_blocks)
    uq = onward(upper_blocks[1])
    u_other = swap(upper_blocks)
    zo, zo_packed = first_inverse(info, diagonal_blocks, d_other)
    zq = onward(zo_packed)
    a, b, vo, go = left_updates(
        info, zo, upper_blocks, u_other, diagonal_blocks, d_other, right_sides, (uq,)
    )
    uqx = swap(uq)
    gq = onward(go, 0, 2)
    zq, a = lax.optimization_barrier((zq, a))
    zqx = swap(zq)
    u_odd, t, ue_full = coupled_upper(info, zq, zqx, upper_blocks, u_other, uq)
    ur = odd_left(u_odd)
    ul = odd_right(u_odd)
    d_mid, u_even, z1, z1_packed = second_inverse(
        info, a, t, ue_full, zq, zqx, upper_blocks, u_other, uq, uqx
    )
    zr = odd_left(z1_packed)
    zl = odd_right(z1_packed)
    f_mid, g1, gt = odd_sources(info, b, gq, ue_full, z1, go, vo, (ur, ul))
    gr = odd_left(g1)
    gl = odd_right(gt)
    urx = swap(ur)
    d_out, u_out, fh, fl, uh, uw = level1_blocks(
        info, d_mid, u_odd, u_even, (ur, urx, zr, swap(zr)), (ul, zl, swap(zl)),
        diagonal_blocks, upper_blocks, u_other,
    )
    f_out = level1_sources(info, f_mid, gr, gl, (fh, fl), (uh, uw), right_sides)
    return d_out, u_out, f_out


def solution(mesh):
    placed = (P("tm", "col", None),) * 3
    return jax.shard_map(body, mesh=mesh, in_specs=placed, out_specs=placed, check_vma=False)
```

```python
import jax
import jax.numpy as jnp
from jax import lax
from jax.experimental import pallas as pl
from jax.experimental.pallas import tpu as pltpu
from jax.sharding import PartitionSpec as P

F32 = jnp.float32
BF16 = jnp.bfloat16
N = 512
H = N // 2

NN = (((1,), (0,)), ((), ()))
NT = (((1,), (1,)), ((), ()))
TN = (((0,), (0,)), ((), ()))

VMEM = pl.BlockSpec(memory_space=pltpu.VMEM)
SMEM = pl.BlockSpec(memory_space=pltpu.SMEM)

SQUARINGS = 4
TARGET = 3e-3
USABLE = 0.6


def dot(a, b, dims=NN):
    return lax.dot_general(a, b, dims, preferred_element_type=F32)


def halves(x):
    high = x.astype(BF16)
    return high, (x - high.astype(F32)).astype(BF16)


def dot3(a, b, dims=NN):
    (ah, al), (bh, bl) = a, b
    return dot(ah, bh, dims) + (dot(ah, bl, dims) + dot(al, bh, dims))


def identity():
    rows = lax.broadcasted_iota(jnp.int32, (N, N), 0)
    lanes = lax.broadcasted_iota(jnp.int32, (N, N), 1)
    return jnp.where(rows == lanes, 1.0, 0.0).astype(F32)


def sweep_inverse(d_ref, x_ref):
    x_ref[...] = d_ref[...]

    def step(k, carry):
        rows = lax.broadcasted_iota(jnp.int32, (N, N), 0)
        lanes = lax.broadcasted_iota(jnp.int32, (N, N), 1)
        a = x_ref[...]
        row = x_ref[pl.ds(k, 1), :]
        col = jnp.sum(jnp.where(lanes == k, a, 0.0), axis=1, keepdims=True)
        lane = lax.broadcasted_iota(jnp.int32, (1, N), 1)
        inv = 1.0 / jnp.sum(jnp.where(lane == k, row, 0.0), axis=1, keepdims=True)
        row = row * inv
        new = a - col * row
        new = jnp.where(rows == k, jnp.broadcast_to(row, (N, N)), new)
        new = jnp.where(lanes == k, jnp.broadcast_to(col * inv, (N, N)), new)
        new = jnp.where(jnp.logical_and(rows == k, lanes == k), -inv, new)
        x_ref[...] = new
        return carry

    lax.fori_loop(0, N, step, 0)
    x_ref[...] = -x_ref[...]


def invert(d_ref, x_ref, res_ref):
    block = d_ref[...]
    low = block.astype(BF16)
    square = dot(low, low)
    top = jnp.max(jnp.sum(jnp.abs(square), axis=1, keepdims=True), axis=0, keepdims=True)
    alpha = 1.9 * lax.rsqrt(top)
    scaled = block * alpha
    y = 2.0 * identity() - scaled
    r = (y - scaled + square * (alpha * alpha) - identity()).astype(BF16)
    for _ in range(SQUARINGS - 1):
        squared = dot(r, r)
        y = y + dot(y.astype(BF16), r)
        r = squared.astype(BF16)
    y = y + dot(y.astype(BF16), r)
    start = (y * alpha).astype(BF16)
    high, rest = halves(d_ref[...])
    residual = identity() - (dot(high, start) + dot(rest, start))
    res_ref[...] = residual
    x_ref[...] = start.astype(F32)
    first = jnp.sum(residual * residual)

    def measure():
        residual = identity() - dot3(halves(d_ref[...]), halves(x_ref[...]))
        res_ref[...] = residual
        return jnp.sum(residual * residual)

    def improve():
        x = x_ref[...]
        x_ref[...] = x + dot(x.astype(BF16), res_ref[...].astype(BF16))

    def going(carry):
        size, count = carry
        return (size > TARGET * TARGET) & (size < USABLE * USABLE) & (count < 6)

    def refine(carry):
        improve()
        return measure(), carry[1] + 1

    size, _ = lax.while_loop(going, refine, (first, 0))
    converged = size <= TARGET * TARGET

    @pl.when(converged)
    def _():
        improve()

    @pl.when(jnp.logical_not(converged))
    def _():
        sweep_inverse(d_ref, x_ref)


def join(info_ref, own_ref, other_ref, full_ref):
    core = info_ref[0]
    full_ref[pl.ds(pl.multiple_of(core * H, H), H), :] = own_ref[...]
    full_ref[pl.ds(pl.multiple_of((1 - core) * H, H), H), :] = other_ref[...]


def own_rows(info_ref, full_ref):
    return full_ref[pl.ds(pl.multiple_of(info_ref[0] * H, H), H), :]


def own_columns(info_ref, full_ref):
    return full_ref[:, pl.ds(pl.multiple_of(info_ref[0] * H, H), H)]


B = 128
PACK = ((0, 0), (1, 0), (1, 1), (2, 0), (2, 1)), ((2, 2), (3, 0), (3, 1), (3, 2), (3, 3))
PACKED = (5 * B, B)


def pack(info_ref, full_ref, out_ref):
    for core in range(2):

        @pl.when(info_ref[0] == core)
        def _():
            for at, (i, j) in enumerate(PACK[core]):
                out_ref[at * B : (at + 1) * B, :] = full_ref[i * B : (i + 1) * B, j * B : (j + 1) * B]


def unpack(info_ref, own_ref, other_ref, full_ref):
    for core in range(2):

        @pl.when(info_ref[0] == core)
        def _():
            for half, ref in ((core, own_ref), (1 - core, other_ref)):
                for at, (i, j) in enumerate(PACK[half]):
                    block = ref[at * B : (at + 1) * B, :]
                    full_ref[i * B : (i + 1) * B, j * B : (j + 1) * B] = block
                    if i != j:
                        full_ref[j * B : (j + 1) * B, i * B : (i + 1) * B] = block.T


CUBE = 2 * N * N * N
FULL = (N, N)
SLAB = (H, N)
PAIR = (2, H, N)


def call(kernel, outs, operands, scratch, cubes, after=(), rounded=(), limit=24):
    count = len(operands)
    outs = [(o, F32) for o in outs] + [(o, BF16) for o in rounded]

    def entry(*refs):
        kernel(*refs[:count], *refs[count + len(after) :])

    return pl.pallas_call(
        entry,
        out_shape=[jax.ShapeDtypeStruct(o, kind) for o, kind in outs],
        in_specs=[SMEM] + [VMEM] * (count - 1) + [pl.BlockSpec(memory_space=pl.ANY)] * len(after),
        out_specs=[VMEM] * len(outs),
        scratch_shapes=[pltpu.VMEM(s, F32) for s in scratch],
        compiler_params=pltpu.CompilerParams(vmem_limit_bytes=limit * 2**20),
        cost_estimate=pl.CostEstimate(
            flops=cubes * CUBE, bytes_accessed=(count + len(outs)) * 4 * H * N, transcendentals=0
        ),
    )(*operands, *after)


def first_inverse(info, d, d_other):
    def kernel(info_ref, own_ref, other_ref, z_ref, zp_ref, d_ref, res_ref):
        join(info_ref, own_ref.at[1], other_ref.at[1], d_ref)
        invert(d_ref, z_ref, res_ref)
        pack(info_ref, z_ref, zp_ref)

    return call(kernel, [FULL, PACKED], [info, d, d_other], [FULL, FULL], 20)


def left_updates(info, z, u, u_other, d, d_other, f, after):
    def kernel(info_ref, z_ref, u_ref, ux_ref, d_ref, dx_ref, f_ref, a_ref, b_ref, v_ref, g_ref, uo_ref):
        join(info_ref, u_ref.at[1], ux_ref.at[1], uo_ref)
        join(info_ref, d_ref.at[0], dx_ref.at[0], a_ref)
        z2 = halves(z_ref[...])
        u2 = halves(uo_ref[...])
        g = dot3(halves(f_ref[1]), z2)
        g_ref[...] = g
        b_ref[...] = f_ref[0] - dot3(halves(g), u2, NT)
        v = dot3(u2, z2)
        v_ref[...] = v
        a_ref[...] = a_ref[...] - dot3(halves(v), u2, NT)

    return call(
        kernel, [FULL, SLAB, FULL, SLAB], [info, z, u, u_other, d, d_other, f], [FULL], 9, after,
    )


def coupled_upper(info, zq, zq_other, u, u_other, uq):
    def kernel(info_ref, zq_ref, zqx_ref, ui_ref, uix_ref, uq_ref, un_ref, t_ref, u_ref, z_ref):
        @pl.when(info_ref[2] > 0)
        def _():
            unpack(info_ref, zq_ref, zqx_ref, z_ref)
            join(info_ref, ui_ref.at[0], uix_ref.at[0], u_ref)
            t = dot3(halves(z_ref[...]), halves(u_ref[...]))
            t_ref[...] = t
            un_ref[...] = -dot3(halves(uq_ref[...]), halves(t))

    return call(kernel, [SLAB, FULL, FULL], [info, zq, zq_other, u, u_other, uq], [FULL], 3)


def second_inverse(info, a, t, u_full, zq, zq_other, u, u_other, uq, uq_other):
    def kernel(
        info_ref, a_ref, t_ref, u_ref, zq_ref, zqx_ref, ui_ref, uix_ref, uq_ref, uqx_ref,
        dc_ref, un_ref, z_ref, zp_ref, d_ref, res_ref,
    ):
        @pl.when(info_ref[2] > 0)
        def _():
            d_ref[...] = a_ref[...] - dot3(halves(u_ref[...]), halves(t_ref[...]), TN)
            dc_ref[...] = own_rows(info_ref, d_ref)
            invert(d_ref, z_ref, res_ref)
            pack(info_ref, z_ref, zp_ref)

        @pl.when(info_ref[2] == 0)
        def _():
            unpack(info_ref, zq_ref, zqx_ref, z_ref)
            join(info_ref, ui_ref.at[0], uix_ref.at[0], d_ref)
            t = halves(dot3(halves(z_ref[...]), halves(d_ref[...])))
            join(info_ref, uq_ref, uqx_ref, z_ref)
            un_ref[...] = jnp.where(info_ref[1] > 0, -dot3(halves(z_ref[...]), t), d_ref[...])
            dc_ref[...] = own_rows(info_ref, a_ref) - dot3(halves(own_columns(info_ref, d_ref)), t, TN)

    return call(
        kernel, [SLAB, FULL, FULL, PACKED], [info, a, t, u_full, zq, zq_other, u, u_other, uq, uq_other],
        [FULL, FULL], 24,
    )


def odd_sources(info, b, gq, u, z, go, v, after):
    def kernel(info_ref, b_ref, gq_ref, u_ref, z_ref, go_ref, v_ref, f_ref, g_ref, gt_ref):
        @pl.when(info_ref[2] > 0)
        def _():
            f = b_ref[...] - dot3(halves(gq_ref[...]), halves(u_ref[...]))
            f_ref[...] = f
            g = dot3(halves(f), halves(z_ref[...]))
            g_ref[...] = g
            gt_ref[...] = go_ref[...] - dot3(halves(g), halves(v_ref[...]))

        @pl.when(info_ref[2] == 0)
        def _():
            f_ref[...] = b_ref[...]

    return call(kernel, [SLAB, SLAB, SLAB], [info, b, gq, u, z, go, v], [], 5, after)


def level1_blocks(info, d, u_odd, mid, right, left, d_in, u_in, u_other):
    ur, urx, zr, zrx = right
    ul, zl, zlx = left

    def kernel(
        info_ref, d_ref, uo_ref, mid_ref, ur_ref, urx_ref, zr_ref, zrx_ref, ul_ref, zl_ref, zlx_ref,
        din_ref, uin_ref, uix_ref, dout_ref, uout_ref, fh_ref, fl_ref, uh_ref, uw_ref, far_ref, z_ref,
    ):
        dout_ref[1] = din_ref[1]
        uout_ref[1] = uin_ref[1]

        @pl.when(info_ref[2] > 0)
        def _():
            dout_ref[0] = d_ref[...]
            uout_ref[0] = uo_ref[...]

        @pl.when(info_ref[2] == 0)
        def _():
            join(info_ref, uin_ref.at[0], uix_ref.at[0], far_ref)
            uh_ref[...], uw_ref[...] = halves(far_ref[...])
            join(info_ref, ur_ref, urx_ref, far_ref)
            far = halves(far_ref[...])
            fh_ref[...], fl_ref[...] = far
            mid = halves(mid_ref[...])
            unpack(info_ref, zr_ref, zrx_ref, z_ref)
            v = dot3(halves(ur_ref[...]), halves(z_ref[...]))
            unpack(info_ref, zl_ref, zlx_ref, z_ref)
            z2 = halves(z_ref[...])
            w = dot3(halves(own_columns(info_ref, mid_ref)), z2, TN)
            dout_ref[0] = d_ref[...] - dot3(halves(v), far, NT) - dot3(halves(w), mid)
            s = dot3(halves(ul_ref[...]), z2)
            fresh = -dot3(halves(s), mid)
            uout_ref[0] = jnp.where(info_ref[1] > 0, fresh, own_rows(info_ref, mid_ref))

    return call(
        kernel, [PAIR, PAIR],
        [info, d, u_odd, mid, ur, urx, zr, zrx, ul, zl, zlx, d_in, u_in, u_other],
        [FULL] * 2, 0, rounded=[FULL] * 4,
    )


def level1_sources(info, f, gl, gr, ue, far, f_in):
    def kernel(info_ref, f_ref, gl_ref, gr_ref, uh_ref, ul_ref, fh_ref, fl_ref, fin_ref, out_ref):
        out_ref[1] = fin_ref[1]

        @pl.when(info_ref[2] > 0)
        def _():
            out_ref[0] = f_ref[...]

        @pl.when(info_ref[2] == 0)
        def _():
            out_ref[0] = (
                f_ref[...]
                - dot3(halves(gr_ref[...]), (fh_ref[...], fl_ref[...]), NT)
                - dot3(halves(gl_ref[...]), (uh_ref[...], ul_ref[...]))
            )

    return call(kernel, [PAIR], [info, f, gl, gr, *ue, *far, f_in], [], 3)[0]


def body(diagonal_blocks, upper_blocks, right_sides):
    chips = lax.axis_size("tm")
    position = lax.axis_index("tm")
    info = jnp.stack([lax.axis_index("col"), (position > 0).astype(jnp.int32), position % 2]).astype(jnp.int32)

    def swap(a):
        return lax.ppermute(a, "col", [(0, 1), (1, 0)])

    def onward(a, first=0, step=1):
        return lax.ppermute(a, "tm", [(i, i + 1) for i in range(first, chips - 1, step)])

    def odd_left(a):
        return lax.ppermute(a, "tm", [(i, i - 1) for i in range(1, chips, 2)])

    def odd_right(a):
        return onward(a, 1, 2)

    d_other = swap(diagonal_blocks)
    uq = onward(upper_blocks[1])
    u_other = swap(upper_blocks)
    zo, zo_packed = first_inverse(info, diagonal_blocks, d_other)
    zq = onward(zo_packed)
    a, b, vo, go = left_updates(
        info, zo, upper_blocks, u_other, diagonal_blocks, d_other, right_sides, (uq,)
    )
    uqx = swap(uq)
    gq = onward(go, 0, 2)
    zq, a = lax.optimization_barrier((zq, a))
    zqx = swap(zq)
    u_odd, t, ue_full = coupled_upper(info, zq, zqx, upper_blocks, u_other, uq)
    ur = odd_left(u_odd)
    ul = odd_right(u_odd)
    d_mid, u_even, z1, z1_packed = second_inverse(
        info, a, t, ue_full, zq, zqx, upper_blocks, u_other, uq, uqx
    )
    zr = odd_left(z1_packed)
    zl = odd_right(z1_packed)
    f_mid, g1, gt = odd_sources(info, b, gq, ue_full, z1, go, vo, (ur, ul))
    gr = odd_left(g1)
    gl = odd_right(gt)
    urx = swap(ur)
    d_out, u_out, fh, fl, uh, uw = level1_blocks(
        info, d_mid, u_odd, u_even, (ur, urx, zr, swap(zr)), (ul, zl, swap(zl)),
        diagonal_blocks, upper_blocks, u_other,
    )
    f_out = level1_sources(info, f_mid, gl, gr, (uh, uw), (fh, fl), right_sides)
    return d_out, u_out, f_out


def solution(mesh):
    placed = (P("tm", "col", None),) * 3
    return jax.shard_map(body, mesh=mesh, in_specs=placed, out_specs=placed, check_vma=False)
```

```python
import jax
import jax.numpy as jnp
from jax import lax
from jax.experimental import pallas as pl
from jax.experimental.pallas import tpu as pltpu
from jax.sharding import PartitionSpec as P

F32 = jnp.float32
BF16 = jnp.bfloat16
N = 512
H = N // 2

NN = (((1,), (0,)), ((), ()))
NT = (((1,), (1,)), ((), ()))
TN = (((0,), (0,)), ((), ()))

VMEM = pl.BlockSpec(memory_space=pltpu.VMEM)
SMEM = pl.BlockSpec(memory_space=pltpu.SMEM)

SQUARINGS = 4
TARGET = 3e-3
USABLE = 0.6


def dot(a, b, dims=NN):
    return lax.dot_general(a, b, dims, preferred_element_type=F32)


def halves(x):
    high = x.astype(BF16)
    return high, (x - high.astype(F32)).astype(BF16)


def dot3(a, b, dims=NN):
    (ah, al), (bh, bl) = a, b
    return dot(ah, bh, dims) + (dot(ah, bl, dims) + dot(al, bh, dims))


def identity():
    rows = lax.broadcasted_iota(jnp.int32, (N, N), 0)
    lanes = lax.broadcasted_iota(jnp.int32, (N, N), 1)
    return jnp.where(rows == lanes, 1.0, 0.0).astype(F32)


def sweep_inverse(d_ref, x_ref):
    x_ref[...] = d_ref[...]

    def step(k, carry):
        rows = lax.broadcasted_iota(jnp.int32, (N, N), 0)
        lanes = lax.broadcasted_iota(jnp.int32, (N, N), 1)
        a = x_ref[...]
        row = x_ref[pl.ds(k, 1), :]
        col = jnp.sum(jnp.where(lanes == k, a, 0.0), axis=1, keepdims=True)
        lane = lax.broadcasted_iota(jnp.int32, (1, N), 1)
        inv = 1.0 / jnp.sum(jnp.where(lane == k, row, 0.0), axis=1, keepdims=True)
        row = row * inv
        new = a - col * row
        new = jnp.where(rows == k, jnp.broadcast_to(row, (N, N)), new)
        new = jnp.where(lanes == k, jnp.broadcast_to(col * inv, (N, N)), new)
        new = jnp.where(jnp.logical_and(rows == k, lanes == k), -inv, new)
        x_ref[...] = new
        return carry

    lax.fori_loop(0, N, step, 0)
    x_ref[...] = -x_ref[...]


def invert(d_ref, x_ref, res_ref):
    block = d_ref[...]
    low = block.astype(BF16)
    square = dot(low, low)
    top = jnp.max(jnp.sum(jnp.abs(square), axis=1, keepdims=True), axis=0, keepdims=True)
    alpha = 1.9 * lax.rsqrt(top)
    scaled = block * alpha
    y = 2.0 * identity() - scaled
    r = (y - scaled + square * (alpha * alpha) - identity()).astype(BF16)
    for _ in range(SQUARINGS - 1):
        squared = dot(r, r)
        y = y + dot(y.astype(BF16), r)
        r = squared.astype(BF16)
    y = y + dot(y.astype(BF16), r)
    start = (y * alpha).astype(BF16)
    high, rest = halves(d_ref[...])
    residual = identity() - (dot(high, start) + dot(rest, start))
    res_ref[...] = residual
    x_ref[...] = start.astype(F32)
    first = jnp.sum(residual * residual)

    def measure():
        residual = identity() - dot3(halves(d_ref[...]), halves(x_ref[...]))
        res_ref[...] = residual
        return jnp.sum(residual * residual)

    def improve():
        x = x_ref[...]
        x_ref[...] = x + dot(x.astype(BF16), res_ref[...].astype(BF16))

    def going(carry):
        size, count = carry
        return (size > TARGET * TARGET) & (size < USABLE * USABLE) & (count < 6)

    def refine(carry):
        improve()
        return measure(), carry[1] + 1

    size, _ = lax.while_loop(going, refine, (first, 0))
    converged = size <= TARGET * TARGET

    @pl.when(converged)
    def _():
        improve()

    @pl.when(jnp.logical_not(converged))
    def _():
        sweep_inverse(d_ref, x_ref)


def join(info_ref, own_ref, other_ref, full_ref):
    core = info_ref[0]
    full_ref[pl.ds(pl.multiple_of(core * H, H), H), :] = own_ref[...]
    full_ref[pl.ds(pl.multiple_of((1 - core) * H, H), H), :] = other_ref[...]


def own_rows(info_ref, full_ref):
    return full_ref[pl.ds(pl.multiple_of(info_ref[0] * H, H), H), :]


def own_columns(info_ref, full_ref):
    return full_ref[:, pl.ds(pl.multiple_of(info_ref[0] * H, H), H)]


B = 128
PACK = ((0, 0), (1, 0), (1, 1), (2, 0), (2, 1)), ((2, 2), (3, 0), (3, 1), (3, 2), (3, 3))
PACKED = (5 * B, B)


def pack(info_ref, full_ref, out_ref):
    for core in range(2):

        @pl.when(info_ref[0] == core)
        def _():
            for at, (i, j) in enumerate(PACK[core]):
                out_ref[at * B : (at + 1) * B, :] = full_ref[i * B : (i + 1) * B, j * B : (j + 1) * B]


def unpack(info_ref, own_ref, other_ref, full_ref):
    for core in range(2):

        @pl.when(info_ref[0] == core)
        def _():
            for half, ref in ((core, own_ref), (1 - core, other_ref)):
                for at, (i, j) in enumerate(PACK[half]):
                    block = ref[at * B : (at + 1) * B, :]
                    full_ref[i * B : (i + 1) * B, j * B : (j + 1) * B] = block
                    if i != j:
                        full_ref[j * B : (j + 1) * B, i * B : (i + 1) * B] = block.T


CUBE = 2 * N * N * N
FULL = (N, N)
SLAB = (H, N)
PAIR = (2, H, N)


def call(kernel, outs, operands, scratch, cubes, after=(), rounded=(), limit=24):
    count = len(operands)
    outs = [(o, F32) for o in outs] + [(o, BF16) for o in rounded]

    def entry(*refs):
        kernel(*refs[:count], *refs[count + len(after) :])

    return pl.pallas_call(
        entry,
        out_shape=[jax.ShapeDtypeStruct(o, kind) for o, kind in outs],
        in_specs=[SMEM] + [VMEM] * (count - 1) + [pl.BlockSpec(memory_space=pl.ANY)] * len(after),
        out_specs=[VMEM] * len(outs),
        scratch_shapes=[pltpu.VMEM(s, F32) for s in scratch],
        compiler_params=pltpu.CompilerParams(vmem_limit_bytes=limit * 2**20),
        cost_estimate=pl.CostEstimate(
            flops=cubes * CUBE, bytes_accessed=(count + len(outs)) * 4 * H * N, transcendentals=0
        ),
    )(*operands, *after)


def first_inverse(info, d, d_other):
    def kernel(info_ref, own_ref, other_ref, z_ref, zp_ref, d_ref, res_ref):
        join(info_ref, own_ref.at[1], other_ref.at[1], d_ref)
        invert(d_ref, z_ref, res_ref)
        pack(info_ref, z_ref, zp_ref)

    return call(kernel, [FULL, PACKED], [info, d, d_other], [FULL, FULL], 20)


def left_updates(info, z, u, u_other, d, d_other, f, after):
    def kernel(info_ref, z_ref, u_ref, ux_ref, d_ref, dx_ref, f_ref, a_ref, b_ref, v_ref, g_ref, uo_ref):
        join(info_ref, u_ref.at[1], ux_ref.at[1], uo_ref)
        join(info_ref, d_ref.at[0], dx_ref.at[0], a_ref)
        z2 = halves(z_ref[...])
        u2 = halves(uo_ref[...])
        g = dot3(halves(f_ref[1]), z2)
        g_ref[...] = g
        b_ref[...] = f_ref[0] - dot3(halves(g), u2, NT)
        v = dot3(u2, z2)
        v_ref[...] = v
        a_ref[...] = a_ref[...] - dot3(halves(v), u2, NT)

    return call(
        kernel, [FULL, SLAB, FULL, SLAB], [info, z, u, u_other, d, d_other, f], [FULL], 9, after,
    )


def coupled_upper(info, zq, zq_other, u, u_other, uq):
    def kernel(info_ref, zq_ref, zqx_ref, ui_ref, uix_ref, uq_ref, un_ref, t_ref, u_ref, z_ref):
        @pl.when(info_ref[2] > 0)
        def _():
            unpack(info_ref, zq_ref, zqx_ref, z_ref)
            join(info_ref, ui_ref.at[0], uix_ref.at[0], u_ref)
            t = dot3(halves(z_ref[...]), halves(u_ref[...]))
            t_ref[...] = t
            un_ref[...] = -dot3(halves(uq_ref[...]), halves(t))

    return call(kernel, [SLAB, FULL, FULL], [info, zq, zq_other, u, u_other, uq], [FULL], 3)


def second_inverse(info, a, t, u_full, zq, zq_other, u, u_other, uq, uq_other):
    def kernel(
        info_ref, a_ref, t_ref, u_ref, zq_ref, zqx_ref, ui_ref, uix_ref, uq_ref, uqx_ref,
        dc_ref, un_ref, z_ref, zp_ref, d_ref, res_ref,
    ):
        @pl.when(info_ref[2] > 0)
        def _():
            d_ref[...] = a_ref[...] - dot3(halves(u_ref[...]), halves(t_ref[...]), TN)
            dc_ref[...] = own_rows(info_ref, d_ref)
            invert(d_ref, z_ref, res_ref)
            pack(info_ref, z_ref, zp_ref)

        @pl.when(info_ref[2] == 0)
        def _():
            unpack(info_ref, zq_ref, zqx_ref, z_ref)
            join(info_ref, ui_ref.at[0], uix_ref.at[0], d_ref)
            t = halves(dot3(halves(z_ref[...]), halves(d_ref[...])))
            join(info_ref, uq_ref, uqx_ref, z_ref)
            un_ref[...] = jnp.where(info_ref[1] > 0, -dot3(halves(z_ref[...]), t), d_ref[...])
            dc_ref[...] = own_rows(info_ref, a_ref) - dot3(halves(own_columns(info_ref, d_ref)), t, TN)

    return call(
        kernel, [SLAB, FULL, FULL, PACKED], [info, a, t, u_full, zq, zq_other, u, u_other, uq, uq_other],
        [FULL, FULL], 24,
    )


def odd_sources(info, b, gq, u, z, go, v, after):
    def kernel(info_ref, b_ref, gq_ref, u_ref, z_ref, go_ref, v_ref, f_ref, g_ref, gt_ref):
        @pl.when(info_ref[2] > 0)
        def _():
            f = b_ref[...] - dot3(halves(gq_ref[...]), halves(u_ref[...]))
            f_ref[...] = f
            g = dot3(halves(f), halves(z_ref[...]))
            g_ref[...] = g
            gt_ref[...] = go_ref[...] - dot3(halves(g), halves(v_ref[...]))

        @pl.when(info_ref[2] == 0)
        def _():
            f_ref[...] = b_ref[...]

    return call(kernel, [SLAB, SLAB, SLAB], [info, b, gq, u, z, go, v], [], 5, after)


def level1_blocks(info, d, u_odd, mid, right, left, d_in, u_in, u_other):
    ur, urx, zr, zrx = right
    ul, zl, zlx = left

    def kernel(
        info_ref, d_ref, uo_ref, mid_ref, ur_ref, urx_ref, zr_ref, zrx_ref, ul_ref, zl_ref, zlx_ref,
        din_ref, uin_ref, uix_ref, dout_ref, uout_ref, fh_ref, fl_ref, uh_ref, uw_ref, far_ref, z_ref,
    ):
        dout_ref[1] = din_ref[1]
        uout_ref[1] = uin_ref[1]

        @pl.when(info_ref[2] > 0)
        def _():
            dout_ref[0] = d_ref[...]
            uout_ref[0] = uo_ref[...]

        @pl.when(info_ref[2] == 0)
        def _():
            join(info_ref, uin_ref.at[0], uix_ref.at[0], far_ref)
            uh_ref[...], uw_ref[...] = halves(far_ref[...])
            join(info_ref, ur_ref, urx_ref, far_ref)
            far = halves(far_ref[...])
            fh_ref[...], fl_ref[...] = halves(far_ref[...].T)
            mid = halves(mid_ref[...])
            unpack(info_ref, zr_ref, zrx_ref, z_ref)
            v = dot3(halves(ur_ref[...]), halves(z_ref[...]))
            unpack(info_ref, zl_ref, zlx_ref, z_ref)
            z2 = halves(z_ref[...])
            w = dot3(halves(own_columns(info_ref, mid_ref)), z2, TN)
            dout_ref[0] = d_ref[...] - dot3(halves(v), far, NT) - dot3(halves(w), mid)
            s = dot3(halves(ul_ref[...]), z2)
            fresh = -dot3(halves(s), mid)
            uout_ref[0] = jnp.where(info_ref[1] > 0, fresh, own_rows(info_ref, mid_ref))

    return call(
        kernel, [PAIR, PAIR],
        [info, d, u_odd, mid, ur, urx, zr, zrx, ul, zl, zlx, d_in, u_in, u_other],
        [FULL] * 2, 0, rounded=[FULL] * 4,
    )


def level1_sources(info, f, gl, gr, ue, far, f_in):
    def kernel(info_ref, f_ref, gl_ref, gr_ref, uh_ref, ul_ref, fh_ref, fl_ref, fin_ref, out_ref):
        out_ref[1] = fin_ref[1]

        @pl.when(info_ref[2] > 0)
        def _():
            out_ref[0] = f_ref[...]

        @pl.when(info_ref[2] == 0)
        def _():
            out_ref[0] = (
                f_ref[...]
                - dot3(halves(gr_ref[...]), (fh_ref[...], fl_ref[...]))
                - dot3(halves(gl_ref[...]), (uh_ref[...], ul_ref[...]))
            )

    return call(kernel, [PAIR], [info, f, gl, gr, *ue, *far, f_in], [], 3)[0]


def body(diagonal_blocks, upper_blocks, right_sides):
    chips = lax.axis_size("tm")
    position = lax.axis_index("tm")
    info = jnp.stack([lax.axis_index("col"), (position > 0).astype(jnp.int32), position % 2]).astype(jnp.int32)

    def swap(a):
        return lax.ppermute(a, "col", [(0, 1), (1, 0)])

    def onward(a, first=0, step=1):
        return lax.ppermute(a, "tm", [(i, i + 1) for i in range(first, chips - 1, step)])

    def odd_left(a):
        return lax.ppermute(a, "tm", [(i, i - 1) for i in range(1, chips, 2)])

    def odd_right(a):
        return onward(a, 1, 2)

    d_other = swap(diagonal_blocks)
    uq = onward(upper_blocks[1])
    u_other = swap(upper_blocks)
    zo, zo_packed = first_inverse(info, diagonal_blocks, d_other)
    zq = onward(zo_packed)
    a, b, vo, go = left_updates(
        info, zo, upper_blocks, u_other, diagonal_blocks, d_other, right_sides, (uq,)
    )
    uqx = swap(uq)
    gq = onward(go, 0, 2)
    zq, a = lax.optimization_barrier((zq, a))
    zqx = swap(zq)
    u_odd, t, ue_full = coupled_upper(info, zq, zqx, upper_blocks, u_other, uq)
    ur = odd_left(u_odd)
    ul = odd_right(u_odd)
    d_mid, u_even, z1, z1_packed = second_inverse(
        info, a, t, ue_full, zq, zqx, upper_blocks, u_other, uq, uqx
    )
    zr = odd_left(z1_packed)
    zl = odd_right(z1_packed)
    f_mid, g1, gt = odd_sources(info, b, gq, ue_full, z1, go, vo, (ur, ul))
    gr = odd_left(g1)
    gl = odd_right(gt)
    urx = swap(ur)
    d_out, u_out, fh, fl, uh, uw = level1_blocks(
        info, d_mid, u_odd, u_even, (ur, urx, zr, swap(zr)), (ul, zl, swap(zl)),
        diagonal_blocks, upper_blocks, u_other,
    )
    f_out = level1_sources(info, f_mid, gl, gr, (uh, uw), (fh, fl), right_sides)
    return d_out, u_out, f_out


def solution(mesh):
    placed = (P("tm", "col", None),) * 3
    return jax.shard_map(body, mesh=mesh, in_specs=placed, out_specs=placed, check_vma=False)
```
